32 devices in a mesh: ctx: 16 (over z, y, x), head: 2 (over core).
Axes of the slice: x: 2, y: 2, z: 4, core: 2. Of those that a mesh axis runs over, the one named last changes fastest.
Arguments:
- lin_query: bfloat16 [4096, 4096], P('ctx', 'head'), may hold values from -200 to 200
- lin_keys: bfloat16 [4096, 4096], P('ctx', 'head'), may hold values from -6 to 6
- lin_values: bfloat16 [4096, 4096], P('ctx', 'head'), may hold values from -6 to 6
- lin_grad: bfloat16 [4096, 4096], P('ctx', 'head'), may hold values from -6 to 6
- norm_gain: float32 [4096], P('head'), may hold values from 0.1 to 1.9
- log_decay: float32 [32, 4096], P('head'), may hold values from -1 to 0, as said below
- state_in: bfloat16 [16, 32, 128, 128], P('ctx', 'head'), may hold values from -96 to 96
- soft_query: bfloat16 [4096, 8192], P('ctx', 'head'), may hold values from -10 to 10
- soft_keys: bfloat16 [4096, 1024], P('ctx', 'head'), may hold values from -4 to 4
- soft_values: bfloat16 [4096, 1024], P('ctx', 'head'), may hold values from -6 to 6
- soft_grad: bfloat16 [4096, 8192], P('ctx', 'head'), may hold values from -6 to 6
- projections: bfloat16 [2, 4096, 1024], P(None, None, 'head'), may hold values from -0.125 to 0.125
- doc_lengths: int32 [8], replicated, may hold values from 1 to 768, 4096 in all
Outputs:
- lin_dq: bfloat16 [4096, 4096], P('ctx', 'head')
- lin_dk: bfloat16 [4096, 4096], P('ctx', 'head')
- lin_dv: bfloat16 [4096, 4096], P('ctx', 'head')
- soft_dq: bfloat16 [4096, 8192], P('ctx', 'head')
- soft_dk: bfloat16 [4096, 1024], P('ctx', 'head')
- soft_dv: bfloat16 [4096, 1024], P('ctx', 'head')
The draws below stay inside these ranges and needn't reach their ends.
Inputs may be any that keep to these rules, and one draw needn't show every extreme that they name: `log_decay`: strictly negative. `doc_lengths`: positive lengths that add up to 4096; the largest is exactly 768.
All inputs are finite; a program needn't handle non-finite values.
Results may differ from the reference program's by a relative error of at most 0.011.
Values may be sent and summed in bfloat16 or wider, within the bound.
A program may use at most 128 MiB of HBM per device.

```python
import math
import jax
import jax.numpy as jnp
import numpy as np
from jax import lax

TOK_DEV = 256
DH = 128
Q_HEADS = 64
KV_HEADS = 8
LIGHTNING_HEADS = 32
SUB = 4
SEQUENCE_LENGTH = 4096
MOST = 768
DOCS = 8
N_CTX = 16


def draw_lin_query(key, part):
    parallel_flows = jax.random.split(jax.random.fold_in(key, 101), 3)
    head_pos = jnp.arange(LIGHTNING_HEADS, dtype=jnp.float32)
    rising = 1.0 + 2.0 * head_pos / max(LIGHTNING_HEADS - 1, 1)
    column_scale = jnp.exp(jax.random.uniform(parallel_flows[1], (LIGHTNING_HEADS, DH), minval=0.0, maxval=jnp.log(4.0)))
    row_scale = jnp.exp(jax.random.uniform(parallel_flows[2], (SEQUENCE_LENGTH, 1, 1), minval=0.0, maxval=jnp.log(3.0)))
    base_draw = jnp.clip(jax.random.normal(parallel_flows[0], (SEQUENCE_LENGTH, LIGHTNING_HEADS, DH)), -4.0, 4.0)
    output_values = base_draw * rising[None, :, None] * column_scale[None] * row_scale
    return output_values.reshape(SEQUENCE_LENGTH, LIGHTNING_HEADS * DH).astype(jnp.bfloat16)


def draw_log_decay(key, part):
    parallel_flows = jax.random.split(jax.random.fold_in(key, 202), 7)
    fast_cut = 5
    fast_heads = jax.random.randint(parallel_flows[0], (LIGHTNING_HEADS,), 0, 10) < fast_cut
    fast_rate = jnp.exp(jax.random.uniform(parallel_flows[1], (LIGHTNING_HEADS,), minval=jnp.log(0.03), maxval=jnp.log(0.08)))
    slow_rate = jax.random.uniform(parallel_flows[2], (LIGHTNING_HEADS,), minval=0.2, maxval=0.6) / SEQUENCE_LENGTH
    per_head_rate = jnp.where(fast_heads, fast_rate, slow_rate)
    block_multiplier = jnp.exp(jax.random.uniform(parallel_flows[3], (LIGHTNING_HEADS, SEQUENCE_LENGTH // TOK_DEV, 1), minval=jnp.log(0.5), maxval=jnp.log(2.0)))
    block_multiplier = jnp.broadcast_to(block_multiplier, (LIGHTNING_HEADS, SEQUENCE_LENGTH // TOK_DEV, TOK_DEV)).reshape(LIGHTNING_HEADS, SEQUENCE_LENGTH)
    local_multiplier = jax.random.uniform(parallel_flows[4], (LIGHTNING_HEADS, SEQUENCE_LENGTH), minval=0.5, maxval=1.5)
    spike_positions = jax.random.randint(parallel_flows[5], (3,), 0, SEQUENCE_LENGTH)
    spike_applied = jnp.any(jnp.arange(SEQUENCE_LENGTH)[:, None] == spike_positions[None, :], axis=1)
    spike_retained = jax.random.uniform(parallel_flows[6], (LIGHTNING_HEADS, SEQUENCE_LENGTH), minval=0.55, maxval=0.8)
    output_values = -per_head_rate[:, None] * block_multiplier * local_multiplier + jnp.where(spike_applied[None, :], jnp.log(spike_retained), 0.0)
    return output_values.astype(jnp.float32)


def softmax_pair(key):
    parallel_flows = jax.random.split(jax.random.fold_in(key, 303), 2)
    query_draw = jnp.clip(jax.random.normal(parallel_flows[0], (SEQUENCE_LENGTH, Q_HEADS, DH)), -4.0, 4.0)
    key_draw = jnp.clip(jax.random.normal(parallel_flows[1], (SEQUENCE_LENGTH, KV_HEADS, DH)), -4.0, 4.0)
    return (query_draw.reshape(SEQUENCE_LENGTH, Q_HEADS * DH), key_draw.reshape(SEQUENCE_LENGTH, KV_HEADS * DH))


def draw_soft_query(key, part):
    return softmax_pair(key)[0].astype(jnp.bfloat16)


def draw_soft_keys(key, part):
    return softmax_pair(key)[1].astype(jnp.bfloat16)


def spiked(values, own_key, source, target, parts, factor):
    def block_of(dim):
        return (jnp.arange(values.shape[dim]) // (values.shape[dim] // parts)).reshape((-1,) + (1,) * (values.ndim - 1 - dim))

    near = jax.random.permutation(own_key, parts)[block_of(target)]
    other_side = (block_of(target) + parts // 2) % parts
    return jnp.where((block_of(source) == near) | (block_of(source) == other_side), factor * values, values)


def steps_of(rng, dims, cuts, least, largest):
    level = 1.0
    for axis_at, blocks in cuts:
        steps = jax.random.uniform(jax.random.fold_in(jax.random.fold_in(rng, 6), axis_at), (blocks,), jnp.float32, least / len(cuts), largest / len(cuts))
        level = level * jnp.repeat(jnp.exp(steps), dims[axis_at] // blocks).reshape((-1,) + (1,) * (len(dims) - 1 - axis_at))
    return level


def split_up(amount, total, limit, lean):
    portions = [(1 << 20) // math.isqrt(grade ** lean) + 1 for grade in range(2, amount + 1)]
    surplus, holding = total - limit - (amount - 1), [1] * (amount - 1)
    while surplus > 0:
        free = [i for i in range(amount - 1) if holding[i] < limit]
        pool, left = sum([portions[i] for i in free]), surplus
        for i in free:
            addition = min(limit - holding[i], max(1, left * portions[i] // pool), surplus)
            holding[i] = holding[i] + addition
            surplus = surplus - addition
    return np.array([limit] + holding)


def uneven(stream_key, amount, total, most, lean):
    if amount == 2:
        one = jax.random.randint(stream_key, (), max(1, total - most), min(most, total - 1) + 1)
        return jnp.stack([one, total - one])
    sizes = jnp.asarray(split_up(amount, total, most, lean), jnp.int32)
    twos = (amount - 1) // 2
    source_of, sink = sizes[1:1 + 2 * twos:2], sizes[2:2 + 2 * twos:2]
    slack = jnp.minimum(source_of - 1, most - sink)
    shifted = jax.random.randint(jax.random.fold_in(stream_key, 1), (twos,), 0, 1 << 20) % (slack + 1)
    sizes = sizes.at[1:1 + 2 * twos:2].set(source_of - shifted).at[2:2 + 2 * twos:2].set(sink + shifted)
    return sizes[jax.random.permutation(jax.random.fold_in(stream_key, 2), amount)]


def gaussian(key, shape, width, bound, pieces=(), held_as=jnp.bfloat16):
    level = steps_of(key, shape, pieces, -0.22, 0.18) if pieces else 1.0
    drawn = jax.random.normal(key, shape, jnp.float32) * width * level
    return jnp.minimum(jnp.maximum(drawn, -bound), bound).astype(held_as)


def noise_with(stream_key, shape, width, most, shards, heavy, kind=jnp.bfloat16):
    values = width * jax.random.normal(stream_key, shape, jnp.float32)
    if shards:
        values = values * steps_of(stream_key, shape, shards, -0.22, 0.18)
    return jnp.clip(spiked(values, jax.random.fold_in(stream_key, 3), *heavy), -most, most).astype(kind)


def setup_inputs(seed: int = 0) -> dict:
    keys = jax.random.split(jax.random.key(seed), 14)
    return {
        "lin_query": draw_lin_query(jax.random.fold_in(keys[13], 71), 0),
        "lin_keys": gaussian(keys[1], (SEQUENCE_LENGTH, LIGHTNING_HEADS * DH), 1.0, 6.0, ((0, 16), (1, 2))),
        "lin_values": gaussian(keys[2], (SEQUENCE_LENGTH, LIGHTNING_HEADS * DH), 1.0, 6.0, ((0, 16), (1, 2))),
        "lin_grad": gaussian(keys[3], (SEQUENCE_LENGTH, LIGHTNING_HEADS * DH), 1.0, 6.0, ((0, 16), (1, 2))),
        "norm_gain": jnp.clip(1.0 + 0.18 * jax.random.normal(keys[4], (LIGHTNING_HEADS * DH,), jnp.float32), 0.1, 1.9),
        "log_decay": draw_log_decay(jax.random.fold_in(keys[13], 71), 0),
        "state_in": gaussian(keys[6], (N_CTX, LIGHTNING_HEADS, DH, DH), 16.0, 96.0, ((0, 16), (1, 2))),
        "soft_query": draw_soft_query(jax.random.fold_in(keys[13], 71), 0),
        "soft_keys": draw_soft_keys(jax.random.fold_in(keys[13], 71), 0),
        "soft_values": gaussian(keys[9], (SEQUENCE_LENGTH, KV_HEADS * DH), 1.0, 6.0, ((0, 16), (1, 2))),
        "soft_grad": gaussian(keys[10], (SEQUENCE_LENGTH, Q_HEADS * DH), 1.0, 6.0, ((0, 16), (1, 2))),
        "projections": noise_with(keys[11], (2, LIGHTNING_HEADS * DH, KV_HEADS * DH), (LIGHTNING_HEADS * DH) ** -0.5, 0.125, ((2, 2),), (2, 1, 2, 2.0)),
        "doc_lengths": uneven(keys[12], DOCS, SEQUENCE_LENGTH, MOST, 2).astype(jnp.int32),
    }


epsilon = 1e-06
precise = lax.Precision.HIGHEST

def document_of(positions, doc_lengths):
    doc_ends = jnp.cumsum(doc_lengths).astype(jnp.int32)
    return lax.optimization_barrier(jnp.sum((doc_ends[None, :] <= positions[:, None]).astype(jnp.int32), axis=1))

def decay_weights(log_block):
    running = jnp.cumsum(log_block, axis=1)
    position = jnp.arange(log_block.shape[1], dtype=jnp.int32)
    before = position[:, None] >= position[None, :]
    log_gap = running[:, :, None] - running[:, None, :]
    weights = jnp.where(before[None], jnp.exp(jnp.minimum(log_gap, 0.0)), 0.0)
    return (running, weights)

def lin_first(query_blk, key_blk, value_blk, grad_blk, gain, log_block, state_blk):
    running, weights = decay_weights(log_block)
    query_f = query_blk.astype(jnp.float32)
    key_f = key_blk.astype(jnp.float32)
    value_f = value_blk.astype(jnp.float32)
    state_f = state_blk.astype(jnp.float32)
    near_terms = (jnp.einsum('thd,shd->hts', query_f, key_f, precision=precise) * weights).astype(jnp.bfloat16)
    near_f = lax.optimization_barrier(near_terms).astype(jnp.float32)
    growth = jnp.exp(running).T[:, :, None]
    scaled_low = (query_f * growth).astype(jnp.bfloat16)
    scaled = lax.optimization_barrier(scaled_low).astype(jnp.float32)
    inside = jnp.einsum('hts,shd->thd', near_f, value_f, precision=precise)
    carried = jnp.einsum('thd,hde->the', scaled, state_f, precision=precise)
    lin_out = (inside + carried) / DH
    gated = gain[None] * grad_blk.astype(jnp.float32)
    features = LIGHTNING_HEADS * DH
    squares = lax.optimization_barrier(jnp.sum(lin_out * lin_out, axis=(1, 2)))
    cross_term = lax.optimization_barrier(jnp.sum(gated * lin_out, axis=(1, 2)))
    spread = jnp.sqrt(squares / features + epsilon)
    out_grad = (gated / spread[:, None, None] - lin_out * (cross_term / (features * spread ** 3))[:, None, None]).astype(jnp.bfloat16)
    out_grad_f = lax.optimization_barrier(out_grad).astype(jnp.float32)
    far_terms = (jnp.einsum('the,she->hts', out_grad_f, value_f, precision=precise) * weights).astype(jnp.bfloat16)
    far_f = lax.optimization_barrier(far_terms).astype(jnp.float32)
    grad_query = (jnp.einsum('hts,shd->thd', far_f, key_f, precision=precise) + growth * jnp.einsum('the,hde->thd', out_grad_f, state_f, precision=precise)) / DH
    summary = jnp.einsum('thd,the->hde', scaled, out_grad_f, precision=precise).astype(jnp.bfloat16)
    return (grad_query.astype(jnp.bfloat16), out_grad, summary, running[:, -1])

def lin_second(query_blk, key_blk, value_blk, out_grad, log_block, after_state):
    running, weights = decay_weights(log_block)
    query_f = query_blk.astype(jnp.float32)
    key_f = key_blk.astype(jnp.float32)
    value_f = value_blk.astype(jnp.float32)
    out_grad_f = out_grad.astype(jnp.float32)
    after_low = lax.optimization_barrier(after_state.astype(jnp.bfloat16)).astype(jnp.float32)
    near_terms = (jnp.einsum('thd,shd->hts', query_f, key_f, precision=precise) * weights).astype(jnp.bfloat16)
    near_f = lax.optimization_barrier(near_terms).astype(jnp.float32)
    far_terms = (jnp.einsum('the,she->hts', out_grad_f, value_f, precision=precise) * weights).astype(jnp.bfloat16)
    far_f = lax.optimization_barrier(far_terms).astype(jnp.float32)
    tail_decay = jnp.exp(running[:, -1:] - running).T[:, :, None]
    grad_key = (jnp.einsum('hst,shd->thd', far_f, query_f, precision=precise) + tail_decay * jnp.einsum('the,hde->thd', value_f, after_low, precision=precise)) / DH
    grad_value = (jnp.einsum('hst,she->the', near_f, out_grad_f, precision=precise) + tail_decay * jnp.einsum('thd,hde->the', key_f, after_low, precision=precise)) / DH
    return (grad_key.astype(jnp.bfloat16), grad_value.astype(jnp.bfloat16))

def lightning_reference(lin_query, lin_keys, lin_values, cotangent, norm_gain, log_decay, state_in):
    block_total = SEQUENCE_LENGTH // TOK_DEV
    shaped = (block_total, TOK_DEV, LIGHTNING_HEADS, DH)
    query_all = lin_query.reshape(shaped)
    key_all = lin_keys.reshape(shaped)
    value_all = lin_values.reshape(shaped)
    grad_all = cotangent.reshape(shaped)
    log_all = log_decay.reshape(LIGHTNING_HEADS, block_total, TOK_DEV).transpose(1, 0, 2)
    gain = norm_gain.reshape(LIGHTNING_HEADS, DH)

    def first_pass(blocks_in):
        return lin_first(blocks_in[0], blocks_in[1], blocks_in[2], blocks_in[3], gain, blocks_in[4], blocks_in[5])
    grad_query, out_grad, summary, totals = lax.map(first_pass, (query_all, key_all, value_all, grad_all, log_all, state_in))

    def backward_step(after_sum, blocks_in):
        block_sum, total_log = blocks_in
        return (block_sum.astype(jnp.float32) + jnp.exp(total_log)[:, None, None] * after_sum, after_sum)
    start_state = jnp.zeros((LIGHTNING_HEADS, DH, DH), jnp.float32)
    last_state, after_all = lax.scan(backward_step, start_state, (summary, totals), reverse=True)

    def second_pass(blocks_in):
        return lin_second(blocks_in[0], blocks_in[1], blocks_in[2], blocks_in[3], blocks_in[4], blocks_in[5])
    grad_key, grad_value = lax.map(second_pass, (query_all, key_all, value_all, out_grad, log_all, after_all))
    flat = (SEQUENCE_LENGTH, LIGHTNING_HEADS * DH)
    return (grad_query.reshape(flat), grad_key.reshape(flat), grad_value.reshape(flat))

def softmax_reference(soft_query, soft_keys, soft_values, soft_grad, doc_lengths):
    group_size = Q_HEADS // KV_HEADS
    window_rows = SUB * TOK_DEV
    margin = (SUB - 1) * TOK_DEV
    score_scale = DH ** (-0.5)
    padding = jnp.zeros((margin, KV_HEADS * DH), jnp.bfloat16)
    key_pad = jnp.concatenate([padding, soft_keys], axis=0)
    value_pad = jnp.concatenate([padding, soft_values], axis=0)

    def one_block(running_sums, block_index):
        acc_key, acc_value = running_sums
        first_row = (block_index * TOK_DEV).astype(jnp.int32)
        query_blk = lax.dynamic_slice_in_dim(soft_query, first_row, TOK_DEV, 0).reshape(TOK_DEV, KV_HEADS, group_size, DH).astype(jnp.float32)
        grad_blk = lax.dynamic_slice_in_dim(soft_grad, first_row, TOK_DEV, 0).reshape(TOK_DEV, KV_HEADS, group_size, DH).astype(jnp.float32)
        key_win = lax.dynamic_slice_in_dim(key_pad, first_row, window_rows, 0).reshape(window_rows, KV_HEADS, DH).astype(jnp.float32)
        value_win = lax.dynamic_slice_in_dim(value_pad, first_row, window_rows, 0).reshape(window_rows, KV_HEADS, DH).astype(jnp.float32)
        query_pos = first_row + jnp.arange(TOK_DEV, dtype=jnp.int32)
        key_pos = first_row - margin + jnp.arange(window_rows, dtype=jnp.int32)
        visible = (key_pos[None, :] <= query_pos[:, None]) & (key_pos[None, :] >= 0) & (document_of(key_pos, doc_lengths)[None, :] == document_of(query_pos, doc_lengths)[:, None])
        scores = jnp.einsum('tkgd,skd->kgts', query_blk, key_win, precision=precise) * score_scale
        scores = jnp.where(visible, scores, -1e+30)
        highest = lax.optimization_barrier(jnp.max(scores, axis=-1, keepdims=True))
        raised = jnp.where(visible, jnp.exp(scores - highest), 0.0)
        attention = raised / lax.optimization_barrier(jnp.sum(raised, axis=-1, keepdims=True))
        prob_low = lax.optimization_barrier(attention.astype(jnp.bfloat16)).astype(jnp.float32)
        output = jnp.einsum('kgts,skd->tkgd', prob_low, value_win, precision=precise)
        row_delta = lax.optimization_barrier(jnp.sum(grad_blk * output, axis=-1))
        grad_probs = jnp.einsum('tkgd,skd->kgts', grad_blk, value_win, precision=precise)
        dscore = (attention * (grad_probs - jnp.transpose(row_delta, (1, 2, 0))[..., None]) * score_scale).astype(jnp.bfloat16)
        dscore_f = lax.optimization_barrier(dscore).astype(jnp.float32)
        grad_query = jnp.einsum('kgts,skd->tkgd', dscore_f, key_win, precision=precise).astype(jnp.bfloat16).reshape(TOK_DEV, Q_HEADS * DH)
        part_key = jnp.einsum('kgts,tkgd->skd', dscore_f, query_blk, precision=precise)
        part_value = jnp.einsum('kgts,tkgd->skd', prob_low, grad_blk, precision=precise)
        acc_key = lax.dynamic_update_slice_in_dim(acc_key, lax.dynamic_slice_in_dim(acc_key, first_row, window_rows, 0) + part_key, first_row, 0)
        acc_value = lax.dynamic_update_slice_in_dim(acc_value, lax.dynamic_slice_in_dim(acc_value, first_row, window_rows, 0) + part_value, first_row, 0)
        return ((acc_key, acc_value), grad_query)
    zero_rows = jnp.zeros((SEQUENCE_LENGTH + margin, KV_HEADS, DH), jnp.float32)
    sums_out, grads = lax.scan(one_block, (zero_rows, zero_rows), jnp.arange(N_CTX, dtype=jnp.int32))
    soft_dq = grads.reshape(SEQUENCE_LENGTH, Q_HEADS * DH)
    soft_dk = sums_out[0][margin:].reshape(SEQUENCE_LENGTH, KV_HEADS * DH).astype(jnp.bfloat16)
    soft_dv = sums_out[1][margin:].reshape(SEQUENCE_LENGTH, KV_HEADS * DH).astype(jnp.bfloat16)
    return (soft_dq, soft_dk, soft_dv)

def reference(lin_query, lin_keys, lin_values, lin_grad, norm_gain, log_decay, state_in, soft_query, soft_keys, soft_values, soft_grad, projections, doc_lengths):
    soft_dq, soft_dk, soft_dv = softmax_reference(soft_query, soft_keys, soft_values, soft_grad, doc_lengths)
    stacked = jnp.stack([soft_dk, soft_dv], axis=1).astype(jnp.float32)
    carried_back = jnp.einsum('tck,cfk->tf', stacked, projections.astype(jnp.float32), precision=precise)
    cotangent = lin_grad.astype(jnp.float32) + carried_back
    lin_dq, lin_dk, lin_dv = lightning_reference(lin_query, lin_keys, lin_values, cotangent, norm_gain, log_decay, state_in)
    return (lin_dq, lin_dk, lin_dv, soft_dq, soft_dk, soft_dv)
```

```python
import functools
import math

import jax
import jax.numpy as jnp
from jax import lax
from jax.experimental import pallas as pl
from jax.experimental.pallas import tpu as pltpu
from jax.sharding import PartitionSpec as P

DH = 128
Q_HEADS = 64
KV_HEADS = 8
LIGHTNING_HEADS = 32
SUB = 4
PAIR = 2

epsilon = 1e-06
precise = lax.Precision.HIGHEST
MESH = pl.DeviceIdType.MESH
LAST = (((1,), (1,)), ((), ()))
FIRST = (((0,), (0,)), ((), ()))
PLAIN = (((1,), (0,)), ((), ()))


def mm(a, b, dims):
    return lax.dot_general(a, b, dims, preferred_element_type=jnp.float32)


def signal(barrier, target):
    pl.semaphore_signal(barrier, inc=1, device_id=target, device_id_type=MESH)


def soft_kernel(
    chain, heads, q, g, k, v, qdoc, kdoc, proj,
    dq, dk, dv, kvg, projall,
    win, bias, acc, own, ret, back,
    win_send, win_recv, ret_send, ret_recv, kvg_send, kvg_recv, proj_send, proj_recv, proj_own,
):
    me = lax.axis_index("ctx")
    hd = lax.axis_index("head")
    L = q.shape[0]
    kvl = k.shape[1] // DH
    group = q.shape[1] // k.shape[1]
    half_rows = L // 2
    W = SUB * L - half_rows
    fl = projall.shape[2]
    own_at = (SUB - 1) * L

    barrier = pltpu.get_barrier_semaphore()
    for d in range(1, SUB):
        @pl.when(me + d < chain)
        def _():
            signal(barrier, {"ctx": me + d})

        @pl.when(me >= d)
        def _():
            signal(barrier, {"ctx": me - d})
    for j in range(1, heads):
        signal(barrier, {"head": lax.rem(hd + j, heads)})
    for c in range(kvl):
        win[0, c, own_at:, :] = k[:, c * DH : (c + 1) * DH]
        win[1, c, own_at:, :] = v[:, c * DH : (c + 1) * DH]
    pl.semaphore_wait(
        barrier, jnp.minimum(me, SUB - 1) + jnp.minimum(chain - 1 - me, SUB - 1) + (heads - 1)
    )

    def window_copy(d, c):
        return pltpu.make_async_remote_copy(
            src_ref=win.at[:, c, pl.ds(own_at, L), :],
            dst_ref=win.at[:, c, pl.ds((SUB - 1 - d) * L, L), :],
            send_sem=win_send.at[d - 1, c],
            recv_sem=win_recv.at[d - 1, c],
            device_id={"ctx": me + d},
            device_id_type=MESH,
        )

    def return_copy(d, c):
        return pltpu.make_async_remote_copy(
            src_ref=ret.at[d - 1, c],
            dst_ref=back.at[d - 1, c],
            send_sem=ret_send.at[d - 1, c],
            recv_sem=ret_recv.at[d - 1, c],
            device_id={"ctx": me - d},
            device_id_type=MESH,
        )

    def proj_copy(j):
        peer = lax.rem(hd + j, heads)
        return pltpu.make_async_remote_copy(
            src_ref=proj.at[:, pl.ds(peer * fl, fl), :],
            dst_ref=projall.at[hd],
            send_sem=proj_send.at[j - 1],
            recv_sem=proj_recv.at[j - 1],
            device_id={"head": peer},
            device_id_type=MESH,
        )

    def kvg_copy(j):
        return pltpu.make_async_remote_copy(
            src_ref=kvg.at[hd],
            dst_ref=kvg.at[hd],
            send_sem=kvg_send.at[j - 1],
            recv_sem=kvg_recv.at[j - 1],
            device_id={"head": lax.rem(hd + j, heads)},
            device_id_type=MESH,
        )

    for c in range(kvl):
        for d in range(1, SUB):
            @pl.when(me + d < chain)
            def _(d=d, c=c):
                window_copy(d, c).start()
    own_proj = pltpu.make_async_copy(proj.at[:, pl.ds(hd * fl, fl), :], projall.at[hd], proj_own)
    own_proj.start()
    for j in range(1, heads):
        proj_copy(j).start()

    for d in range(1, SUB):
        @pl.when(me < d)
        def _(d=d):
            at = (SUB - 1 - d) * L
            win[:, :, at : at + L, :] = jnp.zeros((2, kvl, L, DH), win.dtype)

    for half in range(2):
        r = half * half_rows
        later = lax.broadcasted_iota(jnp.int32, (W, half_rows), 0) - own_at
        row = lax.broadcasted_iota(jnp.int32, (W, half_rows), 1)
        same = kdoc[r : r + W, :] == qdoc[:, r : r + half_rows]
        bias[half] = jnp.where(same & (later <= row), 0.0, -1e30)

    score_scale = DH ** (-0.5)
    to_base2 = score_scale * math.log2(math.e)

    def kv_turn(c, carry):
        for d in range(1, SUB):
            @pl.when(me >= d)
            def _(d=d):
                window_copy(d, c).wait_recv()
        acc[...] = jnp.zeros(acc.shape, acc.dtype)

        def turn(i, inner):
            half = i // (group // PAIR)
            pair = i % (group // PAIR)
            r = pl.multiple_of(half * half_rows, half_rows)
            rows = pl.ds(r, half_rows)
            col = pl.multiple_of((c * group + pair * PAIR) * DH, DH)
            cols = pl.ds(col, PAIR * DH)
            q_wide = q[rows, cols]
            g_wide = g[rows, cols]
            q_rows = jnp.concatenate([q_wide[:, x * DH : (x + 1) * DH] for x in range(PAIR)], 0)
            g_rows = jnp.concatenate([g_wide[:, x * DH : (x + 1) * DH] for x in range(PAIR)], 0)
            k_win = win[0, c, pl.ds(r, W), :]
            v_win = win[1, c, pl.ds(r, W), :]
            b = bias[half]
            s = mm(k_win, q_rows, LAST) * to_base2 + jnp.concatenate([b] * PAIR, 1)
            m = jnp.max(s, axis=0, keepdims=True)
            e = jnp.exp2(s - m)
            total = jnp.sum(e, axis=0, keepdims=True)
            dp = mm(v_win, g_rows, LAST)
            inv = 1.0 / total
            delta = jnp.sum(e * dp, axis=0, keepdims=True) * inv
            p = e * inv
            p_low = p.astype(jnp.bfloat16)
            ds = (p * (dp - delta)).astype(jnp.bfloat16)
            acc[0, pl.ds(r, W), :] += mm(ds, q_rows, PLAIN)
            acc[1, pl.ds(r, W), :] += mm(p_low, g_rows, PLAIN)
            dq_t = mm(k_win, ds, FIRST) * score_scale
            dq_rows = dq_t.T.astype(jnp.bfloat16)
            dq[rows, cols] = jnp.concatenate(
                [dq_rows[x * half_rows : (x + 1) * half_rows] for x in range(PAIR)], 1
            )
            return inner

        lax.fori_loop(0, 2 * (group // PAIR), turn, 0)
        own[0, c] = acc[0, own_at:, :] * score_scale
        own[1, c] = acc[1, own_at:, :]
        for d in range(1, SUB):
            at = (SUB - 1 - d) * L

            @pl.when(me >= d)
            def _(d=d, at=at):
                ret[d - 1, c, 0] = (acc[0, at : at + L, :] * score_scale).astype(ret.dtype)
                ret[d - 1, c, 1] = acc[1, at : at + L, :].astype(ret.dtype)
                return_copy(d, c).start()
        return carry

    lax.fori_loop(0, kvl, kv_turn, 0)

    for c in range(kvl):
        for d in range(1, SUB):
            @pl.when(me + d < chain)
            def _(d=d, c=c):
                return_copy(d, c).wait_recv()
                own[:, c] = own[:, c] + back[d - 1, c].astype(jnp.float32)
        low = own[:, c].astype(jnp.bfloat16)
        kvg[hd, 0, :, c * DH : (c + 1) * DH] = low[0]
        kvg[hd, 1, :, c * DH : (c + 1) * DH] = low[1]
        dk[:, c * DH : (c + 1) * DH] = low[0]
        dv[:, c * DH : (c + 1) * DH] = low[1]
    for j in range(1, heads):
        kvg_copy(j).start()

    for c in range(kvl):
        for d in range(1, SUB):
            @pl.when(me + d < chain)
            def _(d=d, c=c):
                window_copy(d, c).wait_send()

            @pl.when(me >= d)
            def _(d=d, c=c):
                return_copy(d, c).wait_send()
    own_proj.wait()
    for j in range(1, heads):
        proj_copy(j).wait()
    for j in range(1, heads):
        kvg_copy(j).wait()


def document_of(positions, doc_lengths):
    doc_ends = jnp.cumsum(doc_lengths)
    return jnp.sum((doc_ends[None, :] <= positions[:, None]).astype(jnp.int32), axis=1)


def softmax_part(soft_query, soft_keys, soft_values, soft_grad, projections, doc_lengths):
    L = soft_query.shape[0]
    chain = lax.axis_size("ctx")
    heads = lax.axis_size("head")
    kvl = soft_keys.shape[1] // DH
    fl = projections.shape[1] // heads
    first = lax.axis_index("ctx") * L
    query_pos = first + jnp.arange(L, dtype=jnp.int32)
    key_pos = first - (SUB - 1) * L + jnp.arange(SUB * L, dtype=jnp.int32)
    qdoc = document_of(query_pos, doc_lengths)[None, :]
    kdoc = jnp.where(key_pos >= 0, document_of(key_pos, doc_lengths), -1)[:, None]
    half_rows = L // 2
    W = SUB * L - half_rows
    vm = pl.BlockSpec(memory_space=pltpu.VMEM)
    anywhere = pl.BlockSpec(memory_space=pl.ANY)
    bf, f32 = jnp.bfloat16, jnp.float32
    sem = pltpu.SemaphoreType.DMA
    kv_cols = soft_keys.shape[1]
    return pl.pallas_call(
        functools.partial(soft_kernel, chain, heads),
        out_shape=(
            jax.ShapeDtypeStruct(soft_query.shape, bf),
            jax.ShapeDtypeStruct(soft_keys.shape, bf),
            jax.ShapeDtypeStruct(soft_keys.shape, bf),
            jax.ShapeDtypeStruct((heads, 2, L, kv_cols), bf),
            jax.ShapeDtypeStruct((heads, 2, fl, kv_cols), bf),
        ),
        in_specs=[vm] * 6 + [anywhere],
        out_specs=(vm, vm, vm, vm, anywhere),
        scratch_shapes=[
            pltpu.VMEM((2, kvl, SUB * L, DH), bf),
            pltpu.VMEM((2, W, half_rows), f32),
            pltpu.VMEM((2, SUB * L, DH), f32),
            pltpu.VMEM((2, kvl, L, DH), f32),
            pltpu.VMEM((SUB - 1, kvl, 2, L, DH), bf),
            pltpu.VMEM((SUB - 1, kvl, 2, L, DH), bf),
            sem((SUB - 1, kvl)),
            sem((SUB - 1, kvl)),
            sem((SUB - 1, kvl)),
            sem((SUB - 1, kvl)),
            sem((max(1, heads - 1),)),
            sem((max(1, heads - 1),)),
            sem((max(1, heads - 1),)),
            sem((max(1, heads - 1),)),
            sem,
        ],
        compiler_params=pltpu.CompilerParams(
            collective_id=0, has_side_effects=True, vmem_limit_bytes=56 * 1024 * 1024
        ),
        name="softmax_layer",
    )(soft_query, soft_grad, soft_keys, soft_values, qdoc, kdoc, projections)


def decay_weights(log_block):
    running = jnp.cumsum(log_block, axis=1)
    position = jnp.arange(log_block.shape[1], dtype=jnp.int32)
    before = position[:, None] >= position[None, :]
    log_gap = running[:, :, None] - running[:, None, :]
    weights = jnp.where(before[None], jnp.exp(jnp.minimum(log_gap, 0.0)), 0.0)
    return (running, weights)


def lightning_part(lin_query, lin_keys, lin_values, cotangent, norm_gain, log_decay, state_in):
    length = lin_query.shape[0]
    head_count = lin_query.shape[1] // DH
    device = lax.axis_index("ctx")
    chain = lax.axis_size("ctx")
    log_block = lax.dynamic_slice_in_dim(log_decay, device * length, length, 1)
    running, weights = decay_weights(log_block)
    query_blk = lin_query.reshape(length, head_count, DH)
    key_blk = lin_keys.reshape(length, head_count, DH)
    value_blk = lin_values.reshape(length, head_count, DH)
    grad_blk = cotangent.reshape(length, head_count, DH)
    state_blk = state_in[0]
    near_terms = (
        jnp.einsum("thd,shd->hts", query_blk, key_blk, preferred_element_type=jnp.float32) * weights
    ).astype(jnp.bfloat16)
    growth = jnp.exp(running).T[:, :, None]
    scaled = (query_blk.astype(jnp.float32) * growth).astype(jnp.bfloat16)
    inside = jnp.einsum("hts,shd->thd", near_terms, value_blk, preferred_element_type=jnp.float32)
    carried = jnp.einsum("thd,hde->the", scaled, state_blk, preferred_element_type=jnp.float32)
    lin_out = (inside + carried) / DH
    gated = norm_gain.reshape(head_count, DH)[None] * grad_blk
    squares, cross_term = lax.psum(
        (jnp.sum(lin_out * lin_out, axis=(1, 2)), jnp.sum(gated * lin_out, axis=(1, 2))), "head"
    )
    features = LIGHTNING_HEADS * DH
    spread = jnp.sqrt(squares / features + epsilon)
    out_grad = (
        gated / spread[:, None, None]
        - lin_out * (cross_term / (features * spread**3))[:, None, None]
    ).astype(jnp.bfloat16)
    far_terms = (
        jnp.einsum("the,she->hts", out_grad, value_blk, preferred_element_type=jnp.float32)
        * weights
    ).astype(jnp.bfloat16)
    grad_query = (
        jnp.einsum("hts,shd->thd", far_terms, key_blk, preferred_element_type=jnp.float32)
        + growth
        * jnp.einsum("the,hde->thd", out_grad, state_blk, preferred_element_type=jnp.float32)
    ) / DH
    summary = jnp.einsum(
        "thd,the->hde", scaled, out_grad, preferred_element_type=jnp.float32
    ).astype(jnp.bfloat16)
    own_total = running[:, -1]
    totals = jnp.sum(log_decay.reshape(head_count, chain, length), axis=2)
    starts = jnp.concatenate(
        [jnp.zeros((head_count, 1), jnp.float32), jnp.cumsum(totals, axis=1)], axis=1
    )
    anchor = lax.dynamic_slice_in_dim(starts, device + 1, 1, 1)
    block_in = lax.all_gather(summary[None], "ctx", axis=0, tiled=True)
    block_count = block_in.shape[0]
    block_index = jnp.arange(block_count, dtype=jnp.int32)
    log_level = lax.slice_in_dim(starts, 0, block_count, axis=1)
    factors = jnp.where(
        block_index[None, :] > device, jnp.exp(jnp.minimum(log_level - anchor, 0.0)), 0.0
    )
    after_state = jnp.einsum(
        "hn,nhde->hde", factors, block_in.astype(jnp.float32), precision=precise
    )
    after_low = after_state.astype(jnp.bfloat16)
    tail_decay = jnp.exp(own_total[:, None] - running).T[:, :, None]
    grad_key = (
        jnp.einsum("hst,shd->thd", far_terms, query_blk, preferred_element_type=jnp.float32)
        + tail_decay
        * jnp.einsum("the,hde->thd", value_blk, after_low, preferred_element_type=jnp.float32)
    ) / DH
    grad_value = (
        jnp.einsum("hst,she->the", near_terms, out_grad, preferred_element_type=jnp.float32)
        + tail_decay
        * jnp.einsum("thd,hde->the", key_blk, after_low, preferred_element_type=jnp.float32)
    ) / DH
    flat = (length, head_count * DH)
    return (
        grad_query.astype(jnp.bfloat16).reshape(flat),
        grad_key.astype(jnp.bfloat16).reshape(flat),
        grad_value.astype(jnp.bfloat16).reshape(flat),
    )


def per_device(
    lin_query,
    lin_keys,
    lin_values,
    lin_grad,
    norm_gain,
    log_decay,
    state_in,
    soft_query,
    soft_keys,
    soft_values,
    soft_grad,
    projections,
    doc_lengths,
):
    soft_dq, soft_dk, soft_dv, kv_grads, projected = softmax_part(
        soft_query, soft_keys, soft_values, soft_grad, projections, doc_lengths
    )
    carried_back = jnp.einsum(
        "hctk,hcfk->tf", kv_grads, projected, preferred_element_type=jnp.float32
    )
    cotangent = lin_grad.astype(jnp.float32) + carried_back
    lin_dq, lin_dk, lin_dv = lightning_part(
        lin_query, lin_keys, lin_values, cotangent, norm_gain, log_decay, state_in
    )
    return (lin_dq, lin_dk, lin_dv, soft_dq, soft_dk, soft_dv)


def solution(mesh):
    in_specs = (
        P("ctx", "head"),
        P("ctx", "head"),
        P("ctx", "head"),
        P("ctx", "head"),
        P("head"),
        P("head", None),
        P("ctx", "head", None, None),
        P("ctx", "head"),
        P("ctx", "head"),
        P("ctx", "head"),
        P("ctx", "head"),
        P(None, None, "head"),
        P(),
    )
    out_specs = (
        P("ctx", "head"),
        P("ctx", "head"),
        P("ctx", "head"),
        P("ctx", "head"),
        P("ctx", "head"),
        P("ctx", "head"),
    )
    return jax.shard_map(
        per_device, mesh=mesh, in_specs=in_specs, out_specs=out_specs, check_vma=False
    )
```

```python
import functools
import math

import jax
import jax.numpy as jnp
from jax import lax
from jax.experimental import pallas as pl
from jax.experimental.pallas import tpu as pltpu
from jax.sharding import PartitionSpec as P

DH = 128
Q_HEADS = 64
KV_HEADS = 8
LIGHTNING_HEADS = 32
SUB = 4
PAIR = 2

epsilon = 1e-06
MESH = pl.DeviceIdType.MESH
LAST = (((1,), (1,)), ((), ()))
FIRST = (((0,), (0,)), ((), ()))
PLAIN = (((1,), (0,)), ((), ()))


def mm(a, b, dims):
    return lax.dot_general(a, b, dims, preferred_element_type=jnp.float32)


def signal(barrier, target):
    pl.semaphore_signal(barrier, inc=1, device_id=target, device_id_type=MESH)


def soft_kernel(
    chain, heads, q, g, k, v, qdoc, kdoc, proj,
    dq, dk, dv, kvg, projall,
    win, bias, acc, own, ret, back,
    win_send, win_recv, ret_send, ret_recv, kvg_send, kvg_recv, proj_send, proj_recv, proj_own,
):
    me = lax.axis_index("ctx")
    hd = lax.axis_index("head")
    L = q.shape[0]
    kvl = k.shape[1] // DH
    group = q.shape[1] // k.shape[1]
    half_rows = L // 2
    W = SUB * L - half_rows
    fl = projall.shape[2]
    own_at = (SUB - 1) * L

    barrier = pltpu.get_barrier_semaphore()
    for d in range(1, SUB):
        @pl.when(me + d < chain)
        def _():
            signal(barrier, {"ctx": me + d})

        @pl.when(me >= d)
        def _():
            signal(barrier, {"ctx": me - d})
    for j in range(1, heads):
        signal(barrier, {"head": lax.rem(hd + j, heads)})
    for c in range(kvl):
        win[0, c, own_at:, :] = k[:, c * DH : (c + 1) * DH]
        win[1, c, own_at:, :] = v[:, c * DH : (c + 1) * DH]
    pl.semaphore_wait(
        barrier, jnp.minimum(me, SUB - 1) + jnp.minimum(chain - 1 - me, SUB - 1) + (heads - 1)
    )

    def window_copy(d, c):
        return pltpu.make_async_remote_copy(
            src_ref=win.at[:, c, pl.ds(own_at, L), :],
            dst_ref=win.at[:, c, pl.ds((SUB - 1 - d) * L, L), :],
            send_sem=win_send.at[d - 1, c],
            recv_sem=win_recv.at[d - 1, c],
            device_id={"ctx": me + d},
            device_id_type=MESH,
        )

    def return_copy(d, c):
        return pltpu.make_async_remote_copy(
            src_ref=ret.at[d - 1, c],
            dst_ref=back.at[d - 1, c],
            send_sem=ret_send.at[d - 1, c],
            recv_sem=ret_recv.at[d - 1, c],
            device_id={"ctx": me - d},
            device_id_type=MESH,
        )

    def proj_copy(j):
        peer = lax.rem(hd + j, heads)
        return pltpu.make_async_remote_copy(
            src_ref=proj.at[:, pl.ds(peer * fl, fl), :],
            dst_ref=projall.at[hd],
            send_sem=proj_send.at[j - 1],
            recv_sem=proj_recv.at[j - 1],
            device_id={"head": peer},
            device_id_type=MESH,
        )

    def kvg_copy(j):
        return pltpu.make_async_remote_copy(
            src_ref=kvg.at[hd],
            dst_ref=kvg.at[hd],
            send_sem=kvg_send.at[j - 1],
            recv_sem=kvg_recv.at[j - 1],
            device_id={"head": lax.rem(hd + j, heads)},
            device_id_type=MESH,
        )

    for c in range(kvl):
        for d in range(1, SUB):
            @pl.when(me + d < chain)
            def _(d=d, c=c):
                window_copy(d, c).start()
    own_proj = pltpu.make_async_copy(proj.at[:, pl.ds(hd * fl, fl), :], projall.at[hd], proj_own)
    own_proj.start()
    for j in range(1, heads):
        proj_copy(j).start()

    for d in range(1, SUB):
        @pl.when(me < d)
        def _(d=d):
            at = (SUB - 1 - d) * L
            win[:, :, at : at + L, :] = jnp.zeros((2, kvl, L, DH), win.dtype)

    for half in range(2):
        r = half * half_rows
        later = lax.broadcasted_iota(jnp.int32, (W, half_rows), 0) - own_at
        row = lax.broadcasted_iota(jnp.int32, (W, half_rows), 1)
        same = kdoc[r : r + W, :] == qdoc[:, r : r + half_rows]
        bias[half] = jnp.where(same & (later <= row), 0.0, -1e30)

    score_scale = DH ** (-0.5)
    to_base2 = score_scale * math.log2(math.e)

    def kv_turn(c, carry):
        for d in range(1, SUB):
            @pl.when(me >= d)
            def _(d=d):
                window_copy(d, c).wait_recv()
        acc[...] = jnp.zeros(acc.shape, acc.dtype)

        def turn(i, inner):
            half = i // (group // PAIR)
            pair = i % (group // PAIR)
            r = pl.multiple_of(half * half_rows, half_rows)
            rows = pl.ds(r, half_rows)
            col = pl.multiple_of((c * group + pair * PAIR) * DH, DH)
            cols = pl.ds(col, PAIR * DH)
            q_wide = q[rows, cols]
            g_wide = g[rows, cols]
            q_rows = jnp.concatenate([q_wide[:, x * DH : (x + 1) * DH] for x in range(PAIR)], 0)
            g_rows = jnp.concatenate([g_wide[:, x * DH : (x + 1) * DH] for x in range(PAIR)], 0)
            k_win = win[0, c, pl.ds(r, W), :]
            v_win = win[1, c, pl.ds(r, W), :]
            b = bias[half]
            s = mm(k_win, q_rows, LAST) * to_base2 + jnp.concatenate([b] * PAIR, 1)
            m = jnp.max(s, axis=0, keepdims=True)
            e = jnp.exp2(s - m)
            total = jnp.sum(e, axis=0, keepdims=True)
            dp = mm(v_win, g_rows, LAST)
            inv = 1.0 / total
            delta = jnp.sum(e * dp, axis=0, keepdims=True) * inv
            p = e * inv
            p_low = p.astype(jnp.bfloat16)
            ds = (p * (dp - delta)).astype(jnp.bfloat16)
            acc[0, pl.ds(r, W), :] += mm(ds, q_rows, PLAIN)
            acc[1, pl.ds(r, W), :] += mm(p_low, g_rows, PLAIN)
            dq_t = mm(k_win, ds, FIRST) * score_scale
            dq_rows = dq_t.T.astype(jnp.bfloat16)
            dq[rows, cols] = jnp.concatenate(
                [dq_rows[x * half_rows : (x + 1) * half_rows] for x in range(PAIR)], 1
            )
            return inner

        lax.fori_loop(0, 2 * (group // PAIR), turn, 0)
        own[0, c] = acc[0, own_at:, :] * score_scale
        own[1, c] = acc[1, own_at:, :]
        for d in range(1, SUB):
            at = (SUB - 1 - d) * L

            @pl.when(me >= d)
            def _(d=d, at=at):
                ret[d - 1, c, 0] = (acc[0, at : at + L, :] * score_scale).astype(ret.dtype)
                ret[d - 1, c, 1] = acc[1, at : at + L, :].astype(ret.dtype)
                return_copy(d, c).start()
        return carry

    lax.fori_loop(0, kvl, kv_turn, 0)

    for c in range(kvl):
        for d in range(1, SUB):
            @pl.when(me + d < chain)
            def _(d=d, c=c):
                return_copy(d, c).wait_recv()
                own[:, c] = own[:, c] + back[d - 1, c].astype(jnp.float32)
        low = own[:, c].astype(jnp.bfloat16)
        kvg[hd, 0, :, c * DH : (c + 1) * DH] = low[0]
        kvg[hd, 1, :, c * DH : (c + 1) * DH] = low[1]
        dk[:, c * DH : (c + 1) * DH] = low[0]
        dv[:, c * DH : (c + 1) * DH] = low[1]
    for j in range(1, heads):
        kvg_copy(j).start()

    for c in range(kvl):
        for d in range(1, SUB):
            @pl.when(me + d < chain)
            def _(d=d, c=c):
                window_copy(d, c).wait_send()

            @pl.when(me >= d)
            def _(d=d, c=c):
                return_copy(d, c).wait_send()
    own_proj.wait()
    for j in range(1, heads):
        proj_copy(j).wait()
    for j in range(1, heads):
        kvg_copy(j).wait()


def document_of(positions, doc_lengths):
    doc_ends = jnp.cumsum(doc_lengths)
    return jnp.sum((doc_ends[None, :] <= positions[:, None]).astype(jnp.int32), axis=1)


def softmax_part(soft_query, soft_keys, soft_values, soft_grad, projections, doc_lengths):
    L = soft_query.shape[0]
    chain = lax.axis_size("ctx")
    heads = lax.axis_size("head")
    kvl = soft_keys.shape[1] // DH
    fl = projections.shape[1] // heads
    first = lax.axis_index("ctx") * L
    query_pos = first + jnp.arange(L, dtype=jnp.int32)
    key_pos = first - (SUB - 1) * L + jnp.arange(SUB * L, dtype=jnp.int32)
    qdoc = document_of(query_pos, doc_lengths)[None, :]
    kdoc = jnp.where(key_pos >= 0, document_of(key_pos, doc_lengths), -1)[:, None]
    half_rows = L // 2
    W = SUB * L - half_rows
    vm = pl.BlockSpec(memory_space=pltpu.VMEM)
    anywhere = pl.BlockSpec(memory_space=pl.ANY)
    bf, f32 = jnp.bfloat16, jnp.float32
    sem = pltpu.SemaphoreType.DMA
    kv_cols = soft_keys.shape[1]
    return pl.pallas_call(
        functools.partial(soft_kernel, chain, heads),
        out_shape=(
            jax.ShapeDtypeStruct(soft_query.shape, bf),
            jax.ShapeDtypeStruct(soft_keys.shape, bf),
            jax.ShapeDtypeStruct(soft_keys.shape, bf),
            jax.ShapeDtypeStruct((heads, 2, L, kv_cols), bf),
            jax.ShapeDtypeStruct((heads, 2, fl, kv_cols), bf),
        ),
        in_specs=[vm] * 6 + [anywhere],
        out_specs=(vm, vm, vm, vm, anywhere),
        scratch_shapes=[
            pltpu.VMEM((2, kvl, SUB * L, DH), bf),
            pltpu.VMEM((2, W, half_rows), f32),
            pltpu.VMEM((2, SUB * L, DH), f32),
            pltpu.VMEM((2, kvl, L, DH), f32),
            pltpu.VMEM((SUB - 1, kvl, 2, L, DH), bf),
            pltpu.VMEM((SUB - 1, kvl, 2, L, DH), bf),
            sem((SUB - 1, kvl)),
            sem((SUB - 1, kvl)),
            sem((SUB - 1, kvl)),
            sem((SUB - 1, kvl)),
            sem((max(1, heads - 1),)),
            sem((max(1, heads - 1),)),
            sem((max(1, heads - 1),)),
            sem((max(1, heads - 1),)),
            sem,
        ],
        compiler_params=pltpu.CompilerParams(
            collective_id=0, has_side_effects=True, vmem_limit_bytes=56 * 1024 * 1024
        ),
        name="softmax_layer",
    )(soft_query, soft_grad, soft_keys, soft_values, qdoc, kdoc, projections)


def masked_decay(col, row):
    L = col.shape[0]
    at = lax.broadcasted_iota(jnp.int32, (L, L), 0)
    earlier = lax.broadcasted_iota(jnp.int32, (L, L), 1) <= at
    return jnp.where(earlier, jnp.exp(jnp.where(earlier, col - row, 0.0)), 0.0)


def forward_kernel(q, k, v, lg, gain, row, col, state, kvg, proj, out, gated, near, squares, cross):
    weights = masked_decay(col[0], row[0])
    near_low = (mm(q[...], k[...], LAST) * weights).astype(jnp.bfloat16)
    near[0] = near_low
    scaled = (q[...].astype(jnp.float32) * jnp.exp(col[0])).astype(jnp.bfloat16)
    lin_out = (mm(near_low, v[...], PLAIN) + mm(scaled, state[0, 0], PLAIN)) / DH
    cotangent = lg[...].astype(jnp.float32)
    for x in range(kvg.shape[0]):
        for y in range(2):
            cotangent = cotangent + mm(kvg[x, y], proj[x, y], LAST)
    gated_now = gain[...] * cotangent
    out[...] = lin_out
    gated[...] = gated_now

    @pl.when(pl.program_id(0) == 0)
    def _():
        squares[...] = jnp.zeros_like(squares)
        cross[...] = jnp.zeros_like(cross)

    squares[...] += jnp.sum(lin_out * lin_out, axis=1, keepdims=True)
    cross[...] += jnp.sum(gated_now * lin_out, axis=1, keepdims=True)


def norm_kernel(out, gated, squares, cross, q, col, dout, summary):
    features = LIGHTNING_HEADS * DH
    spread = jnp.sqrt(squares[...] / features + epsilon)
    low = (
        gated[...] / spread - out[...] * (cross[...] / (features * spread * spread * spread))
    ).astype(jnp.bfloat16)
    dout[...] = low
    scaled = (q[...].astype(jnp.float32) * jnp.exp(col[0])).astype(jnp.bfloat16)
    summary[0] = mm(scaled, low, FIRST).astype(jnp.bfloat16)


def inner_kernel(q, k, v, dout, near, state, row, col, dq, part_key, part_value):
    weights = masked_decay(col[0], row[0])
    far = (mm(dout[...], v[...], LAST) * weights).astype(jnp.bfloat16)
    carried = mm(dout[...], state[0, 0], LAST)
    dq[...] = ((mm(far, k[...], PLAIN) + jnp.exp(col[0]) * carried) / DH).astype(jnp.bfloat16)
    part_key[...] = mm(far, q[...], FIRST)
    part_value[...] = mm(near[0], dout[...], FIRST)


def outer_kernel(k, v, part_key, part_value, col, after, dk, dv):
    running = col[0]
    tail = jnp.exp(running[running.shape[0] - 1 :, :] - running)
    dk[...] = ((part_key[...] + tail * mm(v[...], after[0], LAST)) / DH).astype(jnp.bfloat16)
    dv[...] = ((part_value[...] + tail * mm(k[...], after[0], PLAIN)) / DH).astype(jnp.bfloat16)


PLANE = 4


def later_states(summary, starts):
    chain = lax.axis_size("ctx")
    groups = chain // PLANE
    me = lax.axis_index("ctx")
    z, j = me // PLANE, me % PLANE
    part = summary.shape[0] // PLANE

    def within(block, d):
        route = [(i, i // PLANE * PLANE + (i + d) % PLANE) for i in range(chain)]
        return lax.ppermute(block, "ctx", route)

    def quarter(array, at):
        return lax.dynamic_slice_in_dim(array, at * part, part, 0)

    pieces = [quarter(summary, j)]
    for d in range(1, PLANE):
        pieces.append(within(quarter(summary, (j + d) % PLANE), d))
    pieces = [piece.astype(jnp.float32) for piece in pieces]
    levels = quarter(starts, j)
    local = lax.dynamic_slice_in_dim(levels, z * PLANE, PLANE + 1, 1)
    source = (j - jnp.arange(PLANE)) % PLANE
    target = (j + jnp.arange(PLANE)) % PLANE
    from_level = jnp.take(local, source, axis=1)
    to_level = jnp.take(local, target + 1, axis=1)
    to_first = jnp.exp(jnp.minimum(from_level - local[:, :1], 0.0))
    factors = jnp.where(
        source[None, :, None] > target[None, None, :],
        jnp.exp(jnp.minimum(from_level[:, :, None] - to_level[:, None, :], 0.0)),
        0.0,
    )
    whole = sum(to_first[:, d, None, None] * pieces[d] for d in range(PLANE))
    whole = whole.astype(jnp.bfloat16)
    carry = jnp.zeros(whole.shape, jnp.float32)
    for e in range(1, groups):
        arrived = lax.ppermute(
            whole, "ctx", [(i, i - PLANE * e) for i in range(PLANE * e, chain)]
        )
        level = lax.dynamic_slice_in_dim(levels, jnp.minimum((z + e) * PLANE, chain), 1, 1)
        decay = jnp.exp(jnp.minimum(level - local[:, PLANE:], 0.0))
        carry = carry + decay[:, :, None] * arrived.astype(jnp.float32)
    last = jnp.exp(jnp.minimum(local[:, PLANE:] - to_level, 0.0))
    result = jnp.zeros(summary.shape, jnp.bfloat16)
    for d in range(PLANE):
        block = last[:, d, None, None] * carry
        for x in range(PLANE):
            block = block + factors[:, x, d, None, None] * pieces[x]
        block = block.astype(jnp.bfloat16)
        if d:
            block = within(block, d)
        result = lax.dynamic_update_slice_in_dim(result, block, (j - d) % PLANE * part, 0)
    return result


def lightning_part(
    lin_query, lin_keys, lin_values, lin_grad, norm_gain, log_decay, state_in, kv_grads, projected
):
    L, width = lin_query.shape
    hl = width // DH
    chain = lax.axis_size("ctx")
    log_block = lax.dynamic_slice_in_dim(log_decay, lax.axis_index("ctx") * L, L, 1)
    running = jnp.cumsum(log_block, axis=1)
    row, col = running[:, None, :], running[:, :, None]
    totals = jnp.sum(log_decay.reshape(hl, chain, L), axis=2)
    starts = jnp.concatenate(
        [jnp.zeros((hl, 1), jnp.float32), jnp.cumsum(totals, axis=1)], axis=1
    )
    bf, f32 = jnp.bfloat16, jnp.float32
    H, _, _, kc = kv_grads.shape
    wide = pl.BlockSpec((L, DH), lambda h: (0, h))
    row_spec = pl.BlockSpec((1, 1, L), lambda h: (h, 0, 0))
    col_spec = pl.BlockSpec((1, L, 1), lambda h: (h, 0, 0))
    state_spec = pl.BlockSpec((1, 1, DH, DH), lambda h: (0, h, 0, 0))
    square_spec = pl.BlockSpec((1, L, L), lambda h: (h, 0, 0))
    matrix_spec = pl.BlockSpec((1, DH, DH), lambda h: (h, 0, 0))
    sum_spec = pl.BlockSpec((L, 1), lambda h: (0, 0))
    shape = jax.ShapeDtypeStruct

    def call(body, name, ins, outs, flops, *args):
        return pl.pallas_call(
            body,
            grid=(hl,),
            in_specs=ins,
            out_specs=tuple(spec for spec, _ in outs),
            out_shape=tuple(kind for _, kind in outs),
            cost_estimate=pl.CostEstimate(
                flops=flops * hl, bytes_accessed=hl * L * DH * 16, transcendentals=hl * L * L
            ),
            compiler_params=pltpu.CompilerParams(vmem_limit_bytes=40 * 1024 * 1024),
            name=name,
        )(*args)

    full_bf, full_f32 = shape((L, width), bf), shape((L, width), f32)
    lin_out, gated, near, squares, cross = call(
        forward_kernel,
        "lightning_forward",
        [
            wide, wide, wide, wide,
            pl.BlockSpec((1, DH), lambda h: (0, h)),
            row_spec, col_spec, state_spec,
            pl.BlockSpec(kv_grads.shape, lambda h: (0, 0, 0, 0)),
            pl.BlockSpec((H, 2, DH, kc), lambda h: (0, 0, h, 0)),
        ],
        [
            (wide, full_f32), (wide, full_f32), (square_spec, shape((hl, L, L), bf)),
            (sum_spec, shape((L, 1), f32)), (sum_spec, shape((L, 1), f32)),
        ],
        2 * L * DH * (2 * L + DH + 2 * H * kc),
        lin_query, lin_keys, lin_values, lin_grad, norm_gain[None, :], row, col, state_in,
        kv_grads, projected,
    )
    squares, cross = lax.psum((squares[:, 0], cross[:, 0]), "head")
    dout, summary = call(
        norm_kernel,
        "norm_backward",
        [wide, wide, sum_spec, sum_spec, wide, col_spec],
        [(wide, full_bf), (matrix_spec, shape((hl, DH, DH), bf))],
        2 * L * DH * DH,
        lin_out, gated, squares[:, None], cross[:, None], lin_query, col,
    )
    after = later_states(summary, starts)
    lin_dq, part_key, part_value = call(
        inner_kernel,
        "lightning_inner",
        [wide, wide, wide, wide, square_spec, state_spec, row_spec, col_spec],
        [(wide, full_bf), (wide, full_f32), (wide, full_f32)],
        2 * L * DH * (4 * L + DH),
        lin_query, lin_keys, lin_values, dout, near, state_in, row, col,
    )
    lin_dk, lin_dv = call(
        outer_kernel,
        "lightning_outer",
        [wide, wide, wide, wide, col_spec, matrix_spec],
        [(wide, full_bf), (wide, full_bf)],
        4 * L * DH * DH,
        lin_keys, lin_values, part_key, part_value, col, after,
    )
    return lin_dq, lin_dk, lin_dv


def per_device(
    lin_query,
    lin_keys,
    lin_values,
    lin_grad,
    norm_gain,
    log_decay,
    state_in,
    soft_query,
    soft_keys,
    soft_values,
    soft_grad,
    projections,
    doc_lengths,
):
    soft_dq, soft_dk, soft_dv, kv_grads, projected = softmax_part(
        soft_query, soft_keys, soft_values, soft_grad, projections, doc_lengths
    )
    lin_dq, lin_dk, lin_dv = lightning_part(
        lin_query, lin_keys, lin_values, lin_grad, norm_gain, log_decay, state_in, kv_grads, projected
    )
    return (lin_dq, lin_dk, lin_dv, soft_dq, soft_dk, soft_dv)


def solution(mesh):
    in_specs = (
        P("ctx", "head"),
        P("ctx", "head"),
        P("ctx", "head"),
        P("ctx", "head"),
        P("head"),
        P("head", None),
        P("ctx", "head", None, None),
        P("ctx", "head"),
        P("ctx", "head"),
        P("ctx", "head"),
        P("ctx", "head"),
        P(None, None, "head"),
        P(),
    )
    out_specs = (
        P("ctx", "head"),
        P("ctx", "head"),
        P("ctx", "head"),
        P("ctx", "head"),
        P("ctx", "head"),
        P("ctx", "head"),
    )
    return jax.shard_map(
        per_device, mesh=mesh, in_specs=in_specs, out_specs=out_specs, check_vma=False
    )
```

```python
import functools
import math

import jax
import jax.numpy as jnp
from jax import lax
from jax.experimental import pallas as pl
from jax.experimental.pallas import tpu as pltpu
from jax.sharding import PartitionSpec as P

DH = 128
Q_HEADS = 64
KV_HEADS = 8
LIGHTNING_HEADS = 32
SUB = 4
PAIR = 4
CHAIN = 2

epsilon = 1e-06
MESH = pl.DeviceIdType.MESH
LAST = (((1,), (1,)), ((), ()))
FIRST = (((0,), (0,)), ((), ()))
PLAIN = (((1,), (0,)), ((), ()))


def mm(a, b, dims):
    return lax.dot_general(a, b, dims, preferred_element_type=jnp.float32)


def signal(barrier, target):
    pl.semaphore_signal(barrier, inc=1, device_id=target, device_id_type=MESH)


def soft_kernel(
    chain, heads, q, g, k, v, qdoc, kdoc, proj,
    dq, dk, dv, kvg, projall,
    win, bias, acc, own, ret, back,
    win_send, win_recv, ret_send, ret_recv, kvg_send, kvg_recv, proj_send, proj_recv, proj_own,
):
    me = lax.axis_index("ctx")
    hd = lax.axis_index("head")
    L = q.shape[0]
    kvl = k.shape[1] // DH
    group = q.shape[1] // k.shape[1]
    half_rows = L // 2
    W = SUB * L - half_rows
    fl = projall.shape[2]
    own_at = (SUB - 1) * L

    barrier = pltpu.get_barrier_semaphore()
    for d in range(1, SUB):
        @pl.when(me + d < chain)
        def _():
            signal(barrier, {"ctx": me + d})

        @pl.when(me >= d)
        def _():
            signal(barrier, {"ctx": me - d})
    for j in range(1, heads):
        signal(barrier, {"head": lax.rem(hd + j, heads)})
    for c in range(kvl):
        win[0, c, own_at:, :] = k[:, c * DH : (c + 1) * DH]
        win[1, c, own_at:, :] = v[:, c * DH : (c + 1) * DH]
    pl.semaphore_wait(
        barrier, jnp.minimum(me, SUB - 1) + jnp.minimum(chain - 1 - me, SUB - 1) + (heads - 1)
    )

    def window_copy(d, c):
        return pltpu.make_async_remote_copy(
            src_ref=win.at[:, c, pl.ds(own_at, L), :],
            dst_ref=win.at[:, c, pl.ds((SUB - 1 - d) * L, L), :],
            send_sem=win_send.at[d - 1, c],
            recv_sem=win_recv.at[d - 1, c],
            device_id={"ctx": me + d},
            device_id_type=MESH,
        )

    def return_copy(d, c):
        return pltpu.make_async_remote_copy(
            src_ref=ret.at[d - 1, c],
            dst_ref=back.at[d - 1, c],
            send_sem=ret_send.at[d - 1, c],
            recv_sem=ret_recv.at[d - 1, c],
            device_id={"ctx": me - d},
            device_id_type=MESH,
        )

    def proj_copy(j):
        peer = lax.rem(hd + j, heads)
        return pltpu.make_async_remote_copy(
            src_ref=proj.at[:, pl.ds(peer * fl, fl), :],
            dst_ref=projall.at[hd],
            send_sem=proj_send.at[j - 1],
            recv_sem=proj_recv.at[j - 1],
            device_id={"head": peer},
            device_id_type=MESH,
        )

    def kvg_copy(j):
        return pltpu.make_async_remote_copy(
            src_ref=kvg.at[hd],
            dst_ref=kvg.at[hd],
            send_sem=kvg_send.at[j - 1],
            recv_sem=kvg_recv.at[j - 1],
            device_id={"head": lax.rem(hd + j, heads)},
            device_id_type=MESH,
        )

    for c in range(kvl):
        for d in range(1, SUB):
            @pl.when(me + d < chain)
            def _(d=d, c=c):
                window_copy(d, c).start()
    own_proj = pltpu.make_async_copy(proj.at[:, pl.ds(hd * fl, fl), :], projall.at[hd], proj_own)
    own_proj.start()
    for j in range(1, heads):
        proj_copy(j).start()

    for d in range(1, SUB):
        @pl.when(me < d)
        def _(d=d):
            at = (SUB - 1 - d) * L
            win[:, :, at : at + L, :] = jnp.zeros((2, kvl, L, DH), win.dtype)

    for half in range(2):
        r = half * half_rows
        later = lax.broadcasted_iota(jnp.int32, (W, half_rows), 0) - own_at
        row = lax.broadcasted_iota(jnp.int32, (W, half_rows), 1)
        same = kdoc[r : r + W, :] == qdoc[:, r : r + half_rows]
        bias[half] = jnp.where(same & (later <= row), 0.0, -1e30)

    score_scale = DH ** (-0.5)
    to_base2 = score_scale * math.log2(math.e)

    def kv_turn(c, carry):
        for d in range(1, SUB):
            @pl.when(me >= d)
            def _(d=d):
                window_copy(d, c).wait_recv()
        acc[...] = jnp.zeros(acc.shape, acc.dtype)

        def turn(i, inner):
            half = i // (group // PAIR)
            pair = i % (group // PAIR)
            r = pl.multiple_of(half * half_rows, half_rows)
            rows = pl.ds(r, half_rows)
            col = pl.multiple_of((c * group + pair * PAIR) * DH, DH)
            cols = pl.ds(col, PAIR * DH)
            q_wide = q[rows, cols]
            g_wide = g[rows, cols]
            q_rows = jnp.concatenate([q_wide[:, x * DH : (x + 1) * DH] for x in range(PAIR)], 0)
            g_rows = jnp.concatenate([g_wide[:, x * DH : (x + 1) * DH] for x in range(PAIR)], 0)
            k_win = win[0, c, pl.ds(r, W), :]
            v_win = win[1, c, pl.ds(r, W), :]
            b = bias[half]
            width = half_rows * CHAIN
            chains = range(0, half_rows * PAIR, width)
            bias_wide = jnp.concatenate([b] * CHAIN, 1)
            scores = [mm(k_win, q_rows[x : x + width], LAST) for x in chains]
            grads = [mm(v_win, g_rows[x : x + width], LAST) for x in chains]
            ds_parts, p_parts = [], []
            for score, dp in zip(scores, grads):
                s = score * to_base2 + bias_wide
                m = jnp.max(s, axis=0, keepdims=True)
                e = jnp.exp2(s - m)
                inv = 1.0 / jnp.sum(e, axis=0, keepdims=True)
                delta = jnp.sum(e * dp, axis=0, keepdims=True) * inv
                p = e * inv
                p_parts.append(p.astype(jnp.bfloat16))
                ds_parts.append((p * (dp - delta)).astype(jnp.bfloat16))
            ds = jnp.concatenate(ds_parts, 1)
            p_low = jnp.concatenate(p_parts, 1)
            acc[0, pl.ds(r, W), :] += mm(ds, q_rows, PLAIN)
            acc[1, pl.ds(r, W), :] += mm(p_low, g_rows, PLAIN)
            dq_t = mm(k_win, ds, FIRST) * score_scale
            dq_rows = dq_t.T.astype(jnp.bfloat16)
            dq[rows, cols] = jnp.concatenate(
                [dq_rows[x * half_rows : (x + 1) * half_rows] for x in range(PAIR)], 1
            )
            return inner

        lax.fori_loop(0, 2 * (group // PAIR), turn, 0)
        own[0, c] = acc[0, own_at:, :] * score_scale
        own[1, c] = acc[1, own_at:, :]
        for d in range(1, SUB):
            at = (SUB - 1 - d) * L

            @pl.when(me >= d)
            def _(d=d, at=at):
                ret[d - 1, c, 0] = (acc[0, at : at + L, :] * score_scale).astype(ret.dtype)
                ret[d - 1, c, 1] = acc[1, at : at + L, :].astype(ret.dtype)
                return_copy(d, c).start()
        return carry

    lax.fori_loop(0, kvl, kv_turn, 0)

    for c in range(kvl):
        for d in range(1, SUB):
            @pl.when(me + d < chain)
            def _(d=d, c=c):
                return_copy(d, c).wait_recv()
                own[:, c] = own[:, c] + back[d - 1, c].astype(jnp.float32)
        low = own[:, c].astype(jnp.bfloat16)
        kvg[hd, 0, :, c * DH : (c + 1) * DH] = low[0]
        kvg[hd, 1, :, c * DH : (c + 1) * DH] = low[1]
        dk[:, c * DH : (c + 1) * DH] = low[0]
        dv[:, c * DH : (c + 1) * DH] = low[1]
    for j in range(1, heads):
        kvg_copy(j).start()

    for c in range(kvl):
        for d in range(1, SUB):
            @pl.when(me + d < chain)
            def _(d=d, c=c):
                window_copy(d, c).wait_send()

            @pl.when(me >= d)
            def _(d=d, c=c):
                return_copy(d, c).wait_send()
    own_proj.wait()
    for j in range(1, heads):
        proj_copy(j).wait()
    for j in range(1, heads):
        kvg_copy(j).wait()


def document_of(positions, doc_lengths):
    doc_ends = jnp.cumsum(doc_lengths)
    return jnp.sum((doc_ends[None, :] <= positions[:, None]).astype(jnp.int32), axis=1)


def softmax_part(soft_query, soft_keys, soft_values, soft_grad, projections, doc_lengths):
    L = soft_query.shape[0]
    chain = lax.axis_size("ctx")
    heads = lax.axis_size("head")
    kvl = soft_keys.shape[1] // DH
    fl = projections.shape[1] // heads
    first = lax.axis_index("ctx") * L
    query_pos = first + jnp.arange(L, dtype=jnp.int32)
    key_pos = first - (SUB - 1) * L + jnp.arange(SUB * L, dtype=jnp.int32)
    qdoc = document_of(query_pos, doc_lengths)[None, :]
    kdoc = jnp.where(key_pos >= 0, document_of(key_pos, doc_lengths), -1)[:, None]
    half_rows = L // 2
    W = SUB * L - half_rows
    vm = pl.BlockSpec(memory_space=pltpu.VMEM)
    anywhere = pl.BlockSpec(memory_space=pl.ANY)
    bf, f32 = jnp.bfloat16, jnp.float32
    sem = pltpu.SemaphoreType.DMA
    kv_cols = soft_keys.shape[1]
    return pl.pallas_call(
        functools.partial(soft_kernel, chain, heads),
        out_shape=(
            jax.ShapeDtypeStruct(soft_query.shape, bf),
            jax.ShapeDtypeStruct(soft_keys.shape, bf),
            jax.ShapeDtypeStruct(soft_keys.shape, bf),
            jax.ShapeDtypeStruct((heads, 2, L, kv_cols), bf),
            jax.ShapeDtypeStruct((heads, 2, fl, kv_cols), bf),
        ),
        in_specs=[vm] * 6 + [anywhere],
        out_specs=(vm, vm, vm, vm, anywhere),
        scratch_shapes=[
            pltpu.VMEM((2, kvl, SUB * L, DH), bf),
            pltpu.VMEM((2, W, half_rows), f32),
            pltpu.VMEM((2, SUB * L, DH), f32),
            pltpu.VMEM((2, kvl, L, DH), f32),
            pltpu.VMEM((SUB - 1, kvl, 2, L, DH), bf),
            pltpu.VMEM((SUB - 1, kvl, 2, L, DH), bf),
            sem((SUB - 1, kvl)),
            sem((SUB - 1, kvl)),
            sem((SUB - 1, kvl)),
            sem((SUB - 1, kvl)),
            sem((max(1, heads - 1),)),
            sem((max(1, heads - 1),)),
            sem((max(1, heads - 1),)),
            sem((max(1, heads - 1),)),
            sem,
        ],
        compiler_params=pltpu.CompilerParams(
            collective_id=0, has_side_effects=True, vmem_limit_bytes=56 * 1024 * 1024
        ),
        name="softmax_layer",
    )(soft_query, soft_grad, soft_keys, soft_values, qdoc, kdoc, projections)


def masked_decay(col, row):
    L = col.shape[0]
    at = lax.broadcasted_iota(jnp.int32, (L, L), 0)
    earlier = lax.broadcasted_iota(jnp.int32, (L, L), 1) <= at
    return jnp.where(earlier, jnp.exp(jnp.where(earlier, col - row, 0.0)), 0.0)


def forward_kernel(q, k, v, lg, gain, row, col, state, kvg, proj, out, gated, near, squares, cross):
    weights = masked_decay(col[0], row[0])
    near_low = (mm(q[...], k[...], LAST) * weights).astype(jnp.bfloat16)
    near[0] = near_low
    scaled = (q[...].astype(jnp.float32) * jnp.exp(col[0])).astype(jnp.bfloat16)
    lin_out = (mm(near_low, v[...], PLAIN) + mm(scaled, state[0, 0], PLAIN)) / DH
    cotangent = lg[...].astype(jnp.float32)
    for x in range(kvg.shape[0]):
        for y in range(2):
            cotangent = cotangent + mm(kvg[x, y], proj[x, y], LAST)
    gated_now = gain[...] * cotangent
    out[...] = lin_out
    gated[...] = gated_now

    @pl.when(pl.program_id(0) == 0)
    def _():
        squares[...] = jnp.zeros_like(squares)
        cross[...] = jnp.zeros_like(cross)

    squares[...] += jnp.sum(lin_out * lin_out, axis=1, keepdims=True)
    cross[...] += jnp.sum(gated_now * lin_out, axis=1, keepdims=True)


def norm_kernel(out, gated, squares, cross, q, col, dout, summary):
    features = LIGHTNING_HEADS * DH
    spread = jnp.sqrt(squares[...] / features + epsilon)
    low = (
        gated[...] / spread - out[...] * (cross[...] / (features * spread * spread * spread))
    ).astype(jnp.bfloat16)
    dout[...] = low
    scaled = (q[...].astype(jnp.float32) * jnp.exp(col[0])).astype(jnp.bfloat16)
    summary[0] = mm(scaled, low, FIRST).astype(jnp.bfloat16)


def inner_kernel(q, k, v, dout, near, state, row, col, dq, part_key, part_value):
    weights = masked_decay(col[0], row[0])
    far = (mm(dout[...], v[...], LAST) * weights).astype(jnp.bfloat16)
    carried = mm(dout[...], state[0, 0], LAST)
    dq[...] = ((mm(far, k[...], PLAIN) + jnp.exp(col[0]) * carried) / DH).astype(jnp.bfloat16)
    part_key[...] = mm(far, q[...], FIRST)
    part_value[...] = mm(near[0], dout[...], FIRST)


def outer_kernel(k, v, part_key, part_value, col, after, dk, dv):
    running = col[0]
    tail = jnp.exp(running[running.shape[0] - 1 :, :] - running)
    dk[...] = ((part_key[...] + tail * mm(v[...], after[0], LAST)) / DH).astype(jnp.bfloat16)
    dv[...] = ((part_value[...] + tail * mm(k[...], after[0], PLAIN)) / DH).astype(jnp.bfloat16)


PLANE = 4


def later_states(summary, totals):
    chain = lax.axis_size("ctx")
    groups = chain // PLANE
    me = lax.axis_index("ctx")
    z, j = me // PLANE, me % PLANE
    part = summary.shape[0] // PLANE

    def within(block, d):
        route = [(i, i // PLANE * PLANE + (i + d) % PLANE) for i in range(chain)]
        return lax.ppermute(block, "ctx", route)

    def quarter(array, at):
        return lax.dynamic_slice_in_dim(array, at * part, part, 0)

    pieces = [quarter(summary, j)]
    for d in range(1, PLANE):
        pieces.append(within(quarter(summary, (j + d) % PLANE), d))
    pieces = [piece.astype(jnp.float32) for piece in pieces]
    ring = jnp.arange(PLANE, dtype=jnp.int32)
    first = z * PLANE
    source = first + (j - ring) % PLANE
    target = first + (j + ring) % PLANE
    beyond = first + PLANE
    farther = beyond + PLANE * jnp.arange(groups, dtype=jnp.int32)
    begins = jnp.concatenate(
        [
            jnp.tile(target + 1, PLANE),
            jnp.full((PLANE,), first),
            target + 1,
            jnp.full((groups,), beyond),
        ]
    )
    ends = jnp.concatenate(
        [jnp.repeat(source, PLANE), source, jnp.full((PLANE,), beyond), farther]
    )
    block = jnp.arange(chain, dtype=jnp.int32)[:, None]
    inside = ((block >= begins) & (block < ends)).astype(jnp.float32)
    log_gap = jnp.sum(quarter(totals, j)[:, :, None] * inside[None], axis=1)
    levels = jnp.where(ends >= begins, jnp.exp(log_gap), 0.0)
    squared = PLANE * PLANE
    factors = levels[:, :squared].reshape(part, PLANE, PLANE)
    to_first = levels[:, squared : squared + PLANE]
    last = levels[:, squared + PLANE : squared + 2 * PLANE]
    decays = levels[:, squared + 2 * PLANE :]
    whole = sum(to_first[:, d, None, None] * pieces[d] for d in range(PLANE))
    whole = whole.astype(jnp.bfloat16)
    carry = jnp.zeros(whole.shape, jnp.float32)
    for e in range(1, groups):
        arrived = lax.ppermute(
            whole, "ctx", [(i, i - PLANE * e) for i in range(PLANE * e, chain)]
        )
        decay = decays[:, e - 1 : e]
        carry = carry + decay[:, :, None] * arrived.astype(jnp.float32)
    result = jnp.zeros(summary.shape, jnp.bfloat16)
    for d in range(PLANE):
        block = last[:, d, None, None] * carry
        for x in range(PLANE):
            block = block + factors[:, x, d, None, None] * pieces[x]
        block = block.astype(jnp.bfloat16)
        if d:
            block = within(block, d)
        result = lax.dynamic_update_slice_in_dim(result, block, (j - d) % PLANE * part, 0)
    return result


def lightning_part(
    lin_query, lin_keys, lin_values, lin_grad, norm_gain, log_decay, state_in, kv_grads, projected
):
    L, width = lin_query.shape
    hl = width // DH
    chain = lax.axis_size("ctx")
    log_block = lax.dynamic_slice_in_dim(log_decay, lax.axis_index("ctx") * L, L, 1)
    running = jnp.cumsum(log_block, axis=1)
    row, col = running[:, None, :], running[:, :, None]
    totals = jnp.sum(log_decay.reshape(hl, chain, L), axis=2)
    bf, f32 = jnp.bfloat16, jnp.float32
    H, _, _, kc = kv_grads.shape
    wide = pl.BlockSpec((L, DH), lambda h: (0, h))
    row_spec = pl.BlockSpec((1, 1, L), lambda h: (h, 0, 0))
    col_spec = pl.BlockSpec((1, L, 1), lambda h: (h, 0, 0))
    state_spec = pl.BlockSpec((1, 1, DH, DH), lambda h: (0, h, 0, 0))
    square_spec = pl.BlockSpec((1, L, L), lambda h: (h, 0, 0))
    matrix_spec = pl.BlockSpec((1, DH, DH), lambda h: (h, 0, 0))
    sum_spec = pl.BlockSpec((L, 1), lambda h: (0, 0))
    shape = jax.ShapeDtypeStruct

    def call(body, name, ins, outs, flops, *args):
        return pl.pallas_call(
            body,
            grid=(hl,),
            in_specs=ins,
            out_specs=tuple(spec for spec, _ in outs),
            out_shape=tuple(kind for _, kind in outs),
            cost_estimate=pl.CostEstimate(
                flops=flops * hl, bytes_accessed=hl * L * DH * 16, transcendentals=hl * L * L
            ),
            compiler_params=pltpu.CompilerParams(vmem_limit_bytes=40 * 1024 * 1024),
            name=name,
        )(*args)

    full_bf, full_f32 = shape((L, width), bf), shape((L, width), f32)
    lin_out, gated, near, squares, cross = call(
        forward_kernel,
        "lightning_forward",
        [
            wide, wide, wide, wide,
            pl.BlockSpec((1, DH), lambda h: (0, h)),
            row_spec, col_spec, state_spec,
            pl.BlockSpec(kv_grads.shape, lambda h: (0, 0, 0, 0)),
            pl.BlockSpec((H, 2, DH, kc), lambda h: (0, 0, h, 0)),
        ],
        [
            (wide, full_f32), (wide, full_f32), (square_spec, shape((hl, L, L), bf)),
            (sum_spec, shape((L, 1), f32)), (sum_spec, shape((L, 1), f32)),
        ],
        2 * L * DH * (2 * L + DH + 2 * H * kc),
        lin_query, lin_keys, lin_values, lin_grad, norm_gain[None, :], row, col, state_in,
        kv_grads, projected,
    )
    squares, cross = lax.psum((squares[:, 0], cross[:, 0]), "head")
    dout, summary = call(
        norm_kernel,
        "norm_backward",
        [wide, wide, sum_spec, sum_spec, wide, col_spec],
        [(wide, full_bf), (matrix_spec, shape((hl, DH, DH), bf))],
        2 * L * DH * DH,
        lin_out, gated, squares[:, None], cross[:, None], lin_query, col,
    )
    after = later_states(summary, totals)
    lin_dq, part_key, part_value = call(
        inner_kernel,
        "lightning_inner",
        [wide, wide, wide, wide, square_spec, state_spec, row_spec, col_spec],
        [(wide, full_bf), (wide, full_f32), (wide, full_f32)],
        2 * L * DH * (4 * L + DH),
        lin_query, lin_keys, lin_values, dout, near, state_in, row, col,
    )
    lin_dk, lin_dv = call(
        outer_kernel,
        "lightning_outer",
        [wide, wide, wide, wide, col_spec, matrix_spec],
        [(wide, full_bf), (wide, full_bf)],
        4 * L * DH * DH,
        lin_keys, lin_values, part_key, part_value, col, after,
    )
    return lin_dq, lin_dk, lin_dv


def per_device(
    lin_query,
    lin_keys,
    lin_values,
    lin_grad,
    norm_gain,
    log_decay,
    state_in,
    soft_query,
    soft_keys,
    soft_values,
    soft_grad,
    projections,
    doc_lengths,
):
    soft_dq, soft_dk, soft_dv, kv_grads, projected = softmax_part(
        soft_query, soft_keys, soft_values, soft_grad, projections, doc_lengths
    )
    lin_dq, lin_dk, lin_dv = lightning_part(
        lin_query, lin_keys, lin_values, lin_grad, norm_gain, log_decay, state_in, kv_grads, projected
    )
    return (lin_dq, lin_dk, lin_dv, soft_dq, soft_dk, soft_dv)


def solution(mesh):
    in_specs = (
        P("ctx", "head"),
        P("ctx", "head"),
        P("ctx", "head"),
        P("ctx", "head"),
        P("head"),
        P("head", None),
        P("ctx", "head", None, None),
        P("ctx", "head"),
        P("ctx", "head"),
        P("ctx", "head"),
        P("ctx", "head"),
        P(None, None, "head"),
        P(),
    )
    out_specs = (
        P("ctx", "head"),
        P("ctx", "head"),
        P("ctx", "head"),
        P("ctx", "head"),
        P("ctx", "head"),
        P("ctx", "head"),
    )
    return jax.shard_map(
        per_device, mesh=mesh, in_specs=in_specs, out_specs=out_specs, check_vma=False
    )
```
